32 devices in a mesh: wire: 8 (over z, y), col: 4 (over x, core).
Axes of the slice: x: 2, y: 2, z: 4, core: 2. Of those that a mesh axis runs over, the one named last changes fastest.
Arguments:
- search: float32 [24576, 384], P('wire', 'col')
- block_values: float32 [24576, 256], P('wire'), may hold values from -0.375 to 0.375
- block_cols: int32 [384, 4], P('wire'), may hold values from 0 to 383, as said below
- ritz: float32 [384, 128], replicated, may hold values from -0.3125 to 0.3125
Outputs:
- new_modes: float32 [24576, 128], P('wire', 'col')
- residual: float32 [24576, 128], P('wire', 'col')
- theta: float32 [128], P('col')
- gram_stiff: float32 [384, 384], P(None, 'col')
- gram_mass: float32 [384, 384], P(None, 'col')
The draws below stay inside these ranges and needn't reach their ends.
Inputs may be any that keep to these rules, and one draw needn't show every extreme that they name: Block rows are in groups of 48, b in group g = b // 48. block_cols[b, 0] = b. Column 1 names a block row of group g. For even b, column 2 names a block row of group g + 1 and column 3 one of group g + 2; for odd b, groups g - 1 and g - 2; groups counted around the loop of all groups.
All inputs are finite; a program needn't handle non-finite values.
Results may differ from the reference program's by a relative error of at most 0.0003.
Values sent between devices are 32-bit elements; how exact they have to be, the bound alone decides.
A program may use at most 64 MiB of HBM per device.

```python
import jax
import jax.numpy as jnp
from jax import lax

BLOCK = 64
SLOTS = 4
MODES = 128
BLK_DEV = 48
SEARCH = 384
NB = 384
NROWS = 24576


def draw_search(key, part):
    first = jax.random.fold_in(key, 0)
    place = jnp.arange(NROWS, dtype=jnp.float32) / jnp.float32(NROWS)
    rising = jnp.sqrt(0.5 + place)
    base = jax.random.normal(first, (NROWS, SEARCH), jnp.float32)
    values = base * rising[:, None]
    return jnp.clip(values, -12.0, 12.0).astype(jnp.float32)


def draw_block_cols(key, part):
    key_one, key_two = jax.random.split(key, 2)
    groups = NB // BLK_DEV
    rows = jnp.arange(NB, dtype=jnp.int32)
    owner = rows // BLK_DEV
    same = owner * BLK_DEV + jax.random.randint(key_one, (NB,), 0, BLK_DEV).astype(jnp.int32)
    sign = 1 - 2 * (rows % 2)
    reach = jnp.stack([sign, 2 * sign], axis=1).astype(jnp.int32)
    target = (owner[:, None] + reach + groups) % groups
    remote = target * BLK_DEV + jax.random.randint(key_two, (NB, 2), 0, BLK_DEV).astype(jnp.int32)
    return jnp.concatenate([rows[:, None], same[:, None], remote], axis=1).astype(jnp.int32)


def block_levels(key, shape, cuts, least, high):
    def one(dim, parts):
        draws = jax.random.uniform(jax.random.fold_in(jax.random.fold_in(key, 6), dim), (parts,), jnp.float32, least / len(cuts), high / len(cuts))
        return jnp.repeat(jnp.exp(draws), shape[dim] // parts).reshape((-1,) + (1,) * (len(shape) - dim - 1))

    loudness = one(*cuts[0])
    for cut in cuts[1:]:
        loudness = loudness * one(*cut)
    return loudness


def scatter_about(key, extent, scale, most, shards=(), kind=jnp.bfloat16):
    level = block_levels(key, extent, shards, -0.22, 0.18) if shards else 1.0
    values = jax.random.normal(key, extent, jnp.float32) * scale * level
    return jnp.minimum(jnp.maximum(values, -most), most).astype(kind)


def setup_inputs(seed: int = 0) -> dict:
    keys = jax.random.split(jax.random.key(seed), 5)
    return {
        "search": draw_search(jax.random.fold_in(keys[4], 71), 0),
        "block_values": scatter_about(keys[1], (NROWS, SLOTS * BLOCK), (SLOTS * BLOCK) ** -0.5, 0.375, ((0, 8),), jnp.float32),
        "block_cols": draw_block_cols(jax.random.fold_in(keys[4], 71), 0),
        "ritz": scatter_about(keys[3], (SEARCH, MODES), SEARCH ** -0.5, 0.3125, (), jnp.float32),
    }


def reference(search, block_values, block_cols, ritz):
    high = lax.Precision.HIGHEST
    blocks = search.reshape(NB, BLOCK, SEARCH)
    groups = NB // BLK_DEV
    values = block_values.reshape(groups, BLK_DEV, BLOCK, SLOTS * BLOCK)
    columns = block_cols.reshape(groups, BLK_DEV, SLOTS)

    def one_group(pair):
        group_values, group_cols = pair
        picked = blocks[group_cols].reshape(BLK_DEV, SLOTS * BLOCK, SEARCH)
        return jnp.einsum("bik,bkc->bic", group_values, picked, precision=high)

    product = lax.map(one_group, (values, columns)).reshape(NROWS, SEARCH)
    image = 4.0 * search + product
    gram_stiff = jnp.einsum("rk,rc->kc", search, image, precision=high) / jnp.float32(NROWS)
    gram_mass = jnp.einsum("rk,rc->kc", search, search, precision=high) / jnp.float32(NROWS)
    new_modes = jnp.dot(search, ritz, precision=high, preferred_element_type=jnp.float32)
    new_image = jnp.dot(image, ritz, precision=high, preferred_element_type=jnp.float32)
    numer = jnp.sum(new_modes * new_image, axis=0)
    denom = jnp.sum(new_modes * new_modes, axis=0)
    theta = numer / denom
    residual = new_image - new_modes * theta[None, :]
    return (new_modes, residual, theta, gram_stiff, gram_mass)
```

```python
import functools

import jax
import jax.numpy as jnp
from jax import lax
from jax.experimental import pallas as pl
from jax.experimental.pallas import tpu as pltpu
from jax.sharding import PartitionSpec as P

MESH = pl.DeviceIdType.MESH
DISTANCES = (1, 2, -1, -2)
NN = (((1,), (0,)), ((), ()))
NT = (((1,), (1,)), ((), ()))


def split(x):
    high = x.astype(jnp.bfloat16)
    return high, (x - high.astype(jnp.float32)).astype(jnp.bfloat16)


def product(a, b, dims=NN):
    mul = functools.partial(lax.dot_general, dimension_numbers=dims, preferred_element_type=jnp.float32)
    return mul(a[0], b[0]) + (mul(a[0], b[1]) + mul(a[1], b[0]))


def remote(src, dst, send, recv, device):
    return pltpu.make_async_remote_copy(
        src_ref=src, dst_ref=dst, send_sem=send, recv_sem=recv, device_id=device, device_id_type=MESH
    )


def kernel(
    nw, nc, parts, total_rows,
    asked, near, search, values, rcols, rmine,
    modes_out, resid_out, theta_out, grams_out,
    stage, halo, others, st_hi, st_lo, image, part, got, gram, gram_got, gram_full, terms, terms_got,
    halo_send, halo_recv, all_send, all_recv, sum_send, sum_recv,
    red_send, red_recv, bc_send, bc_recv, th_send, th_recv,
):
    blk, block, width = search.shape
    half = blk // 2
    wide = gram.shape[1]
    mc = rcols.shape[0]
    rows = blk * block
    span = rows // parts
    bspan = blk // parts
    hspan = half // parts
    chunk = gram_got.shape[2]
    owners = wide // chunk
    w = lax.axis_index("wire")
    c = lax.axis_index("col")

    def on_wire(k):
        return lax.rem(w + k + nw, nw)

    def on_col(k):
        return lax.rem(c + k + nc, nc)

    barrier = pltpu.get_barrier_semaphore()

    @pl.loop(1, nw)
    def _(k):
        pl.semaphore_signal(barrier, inc=1, device_id={"wire": on_wire(k)}, device_id_type=MESH)

    for k in range(1, nc):
        pl.semaphore_signal(barrier, inc=1, device_id={"col": on_col(k)}, device_id_type=MESH)

    def fetch(t):
        @pl.loop(t * hspan, (t + 1) * hspan)
        def _(j):
            for d in range(4):
                stage[d, j] = search[asked[d, j]]

    def halo_copy(d, t):
        js = pl.ds(t * hspan, hspan)
        return remote(
            stage.at[d, js], halo.at[d, js], halo_send.at[d, t], halo_recv.at[d, t],
            {"wire": on_wire(-DISTANCES[d])},
        )

    def all_copy(k):
        return remote(search, others.at[c], all_send.at[k - 1], all_recv.at[k - 1], {"col": on_col(k)})

    def all_arrival(k):
        return remote(
            search, others.at[on_col(-k)], all_send.at[k - 1], all_recv.at[k - 1], {"col": on_col(k)}
        )

    def sum_copy(k, t):
        ls = pl.ds(t * span, span)
        return remote(
            part.at[on_col(k), :, ls], got.at[k - 1, :, ls],
            sum_send.at[k - 1, t], sum_recv.at[k - 1, t], {"col": on_col(k)},
        )

    def red_copy(g, k):
        p = on_wire(k)
        first = pl.multiple_of(lax.rem(p, owners) * chunk, 8)
        return remote(
            gram.at[g, pl.ds(first, chunk)], gram_got.at[g, k],
            red_send.at[g, k], red_recv.at[g, k], {"wire": p},
        )

    def start_red(g):
        @pl.loop(1, nw)
        def _(k):
            if owners == nw:
                red_copy(g, k).start()
            else:
                @pl.when(on_wire(k) < owners)
                def _():
                    red_copy(g, k).start()

    def bc_copy(k, origin):
        first = pl.multiple_of(lax.rem(origin, owners) * chunk, 8)
        view = gram_full.at[:, pl.ds(first, chunk)]
        return remote(view, view, bc_send.at[k], bc_recv.at[k], {"wire": on_wire(k)})

    def th_copy(k):
        return remote(terms, terms_got.at[k], th_send.at[k], th_recv.at[k], {"wire": on_wire(k)})

    fetch(0)
    others[c] = search[...]
    pl.semaphore_wait(barrier, nw + nc - 2)
    for t in range(parts):
        if t > 0:
            fetch(t)
        for d in (3, 1, 0, 2):
            halo_copy(d, t).start()
    for k in range(1, nc):
        all_copy(k).start()

    def turn(q):
        @pl.loop(0, parts)
        def _(t):
            at = others[q, pl.ds(t * bspan, bspan)].reshape(span, width).T
            high, low = split(at)
            ls = pl.ds(pl.multiple_of(t * span, 128), span)
            rs = pl.ds(pl.multiple_of(q * width, 16), width)
            st_hi[rs, ls] = high
            st_lo[rs, ls] = low

    turn(c)
    for k in range(1, nc):
        all_arrival(k).wait_recv()
        turn(on_col(-k))

    rc = split(rcols[...])
    gram[...] = jnp.zeros_like(gram)

    @pl.loop(0, parts)
    def _(t):
        ls = pl.ds(pl.multiple_of(t * span, 128), span)
        here = (st_hi[:, ls], st_lo[:, ls])
        own = split(search[pl.ds(t * bspan, bspan)].reshape(span, width))
        gram[1] += product(here, own)
        modes_out[:, ls] = product(rc, here)

    start_red(1)

    rm = split(rmine[...])
    for t in range(parts):
        for d in range(4):
            halo_copy(d, t).wait_recv()

        @pl.loop(t * hspan, (t + 1) * hspan)
        def _(j):
            for odd in range(2):
                i = 2 * j + odd
                picked = jnp.concatenate(
                    [search[i], search[near[i]], halo[2 * odd, j], halo[2 * odd + 1, j]], axis=0
                )
                image[i] = 4.0 * search[i] + product(split(values[i]), split(picked))

        img = split(image[t * bspan:(t + 1) * bspan].reshape(span, width))
        turned = product(rm, img, NT)
        for q in range(nc):
            part[q, :, t * span:(t + 1) * span] = turned[q * mc:(q + 1) * mc]
        for k in range(1, nc):
            sum_copy(k, t).start()
        here = (st_hi[:, t * span:(t + 1) * span], st_lo[:, t * span:(t + 1) * span])
        gram[0] += product(here, img)

    start_red(0)

    numer = jnp.zeros((mc, 1), jnp.float32)
    denom = jnp.zeros((mc, 1), jnp.float32)
    for t in range(parts):
        ls = slice(t * span, (t + 1) * span)
        for k in range(1, nc):
            sum_copy(k, t).wait_recv()
        mine = part[c, :, ls]
        for k in range(1, nc):
            mine = mine + got[k - 1, :, ls]
        resid_out[:, ls] = mine
        modes = modes_out[:, ls]
        numer = numer + jnp.sum(modes * mine, axis=1, keepdims=True)
        denom = denom + jnp.sum(modes * modes, axis=1, keepdims=True)
    lane = lax.broadcasted_iota(jnp.int32, terms.shape, 1)
    terms[...] = jnp.where(lane < 64, numer, denom)

    @pl.loop(1, nw)
    def _(k):
        th_copy(k).start()

    def own_chunk():
        first = pl.multiple_of(lax.rem(w, owners) * chunk, 8)
        for g in range(2):
            gram_got[g, 0] = gram[g, pl.ds(first, chunk)]

            @pl.loop(1, nw)
            def _(k):
                red_copy(g, k).wait_recv()
                gram_got[g, 0] += gram_got[g, k]

            gram_full[g, pl.ds(first, chunk)] = gram_got[g, 0] * (1.0 / total_rows)

        @pl.loop(1, nw)
        def _(k):
            bc_copy(k, w).start()

    if owners == nw:
        own_chunk()
    else:
        pl.when(w < owners)(own_chunk)

    terms_got[0] = terms[...]

    @pl.loop(1, nw)
    def _(k):
        th_copy(k).wait_recv()
        terms_got[0] += terms_got[k]

    sums = terms_got[0]
    theta = sums[:, 0:1] / sums[:, 64:65]
    theta_out[...] = jnp.broadcast_to(theta, theta_out.shape)
    resid_out[...] = resid_out[...] - modes_out[...] * theta

    @pl.loop(1, nw)
    def _(k):
        th_copy(k).wait_send()
        if owners == nw:
            bc_copy(k, on_wire(-k)).wait_recv()
            bc_copy(k, w).wait_send()
            red_copy(0, k).wait_send()
            red_copy(1, k).wait_send()
        else:
            @pl.when(on_wire(-k) < owners)
            def _():
                bc_copy(k, on_wire(-k)).wait_recv()

            @pl.when(w < owners)
            def _():
                bc_copy(k, w).wait_send()

            @pl.when(on_wire(k) < owners)
            def _():
                red_copy(0, k).wait_send()
                red_copy(1, k).wait_send()

    grams_out[...] = gram_full[...]
    for t in range(parts):
        for d in range(4):
            halo_copy(d, t).wait_send()
        for k in range(1, nc):
            sum_copy(k, t).wait_send()
    for k in range(1, nc):
        all_copy(k).wait_send()


def shards(search, block_values, block_cols, ritz):
    rows, width = search.shape
    blk, slots = block_cols.shape
    assert blk % 2 == 0 and slots == 4
    block = rows // blk
    half = blk // 2
    wide, modes = ritz.shape
    nw, nc = lax.axis_size("wire"), lax.axis_size("col")
    mc = modes // nc
    c = lax.axis_index("col")
    parts = next(n for n in (3, 2, 1) if half % n == 0 and (rows // n) % 128 == 0)
    chunk = max(8, -(-wide // nw) // 8 * 8)
    assert wide % chunk == 0 and wide // chunk <= nw
    owners = wide // chunk
    local = block_cols % blk
    asked = []
    for distance, wanted in zip(
        DISTANCES, (local[0::2, 2], local[0::2, 3], local[1::2, 2], local[1::2, 3])
    ):
        asked.append(lax.ppermute(wanted, "wire", [(i, (i + distance) % nw) for i in range(nw)]))
    asked = jnp.stack(asked)
    rcols = lax.dynamic_slice_in_dim(ritz, c * mc, mc, 1).T
    rmine = lax.dynamic_slice_in_dim(ritz, c * width, width, 0).T
    f32 = jnp.float32
    vmem = pl.BlockSpec(memory_space=pltpu.VMEM)
    smem = pl.BlockSpec(memory_space=pltpu.SMEM)
    dma = pltpu.SemaphoreType.DMA
    modes_t, resid_t, theta, grams = pl.pallas_call(
        functools.partial(kernel, nw, nc, parts, float(rows * nw)),
        out_shape=(
            jax.ShapeDtypeStruct((mc, rows), f32),
            jax.ShapeDtypeStruct((mc, rows), f32),
            jax.ShapeDtypeStruct((mc, 128), f32),
            jax.ShapeDtypeStruct((2, wide, width), f32),
        ),
        in_specs=[smem, smem, vmem, vmem, vmem, vmem],
        out_specs=(vmem,) * 4,
        scratch_shapes=[
            pltpu.VMEM((4, half, block, width), f32),
            pltpu.VMEM((4, half, block, width), f32),
            pltpu.VMEM((nc, blk, block, width), f32),
            pltpu.VMEM((wide, rows), jnp.bfloat16),
            pltpu.VMEM((wide, rows), jnp.bfloat16),
            pltpu.VMEM((blk, block, width), f32),
            pltpu.VMEM((nc, mc, rows), f32),
            pltpu.VMEM((nc - 1, mc, rows), f32),
            pltpu.VMEM((2, wide, width), f32),
            pltpu.VMEM((2, nw, chunk, width), f32),
            pltpu.VMEM((2, wide, width), f32),
            pltpu.VMEM((mc, 128), f32),
            pltpu.VMEM((nw, mc, 128), f32),
            dma((4, parts)), dma((4, parts)),
            dma((nc - 1,)), dma((nc - 1,)),
            dma((nc - 1, parts)), dma((nc - 1, parts)),
            dma((2, nw)), dma((2, nw)),
            dma((nw,)), dma((nw,)),
            dma((nw,)), dma((nw,)),
        ],
        compiler_params=pltpu.CompilerParams(
            collective_id=0, has_side_effects=True, vmem_limit_bytes=56 * 1024 * 1024
        ),
        name="step",
    )(asked, local[:, 1], search.reshape(blk, block, width),
      block_values.reshape(blk, block, slots * block), rcols, rmine)
    return modes_t.T, resid_t.T, theta[:, 0], grams[0], grams[1]


def solution(mesh):
    placed = (P("wire", "col"), P("wire", None), P("wire", None), P())
    return jax.shard_map(
        shards,
        mesh=mesh,
        in_specs=placed,
        out_specs=(P("wire", "col"), P("wire", "col"), P("col"), P(None, "col"), P(None, "col")),
        check_vma=False,
    )
```

```python
import functools

import jax
import jax.numpy as jnp
from jax import lax
from jax.experimental import pallas as pl
from jax.experimental.pallas import tpu as pltpu
from jax.sharding import PartitionSpec as P

MESH = pl.DeviceIdType.MESH
DISTANCES = (1, 2, -1, -2)
NN = (((1,), (0,)), ((), ()))
NT = (((1,), (1,)), ((), ()))


def split(x):
    high = x.astype(jnp.bfloat16)
    return high, (x - high.astype(jnp.float32)).astype(jnp.bfloat16)


def product(a, b, dims=NN):
    mul = functools.partial(lax.dot_general, dimension_numbers=dims, preferred_element_type=jnp.float32)
    return mul(a[0], b[0]) + (mul(a[0], b[1]) + mul(a[1], b[0]))


def remote(src, dst, send, recv, device):
    return pltpu.make_async_remote_copy(
        src_ref=src, dst_ref=dst, send_sem=send, recv_sem=recv, device_id=device, device_id_type=MESH
    )


def kernel(
    nw, nc, parts, total_rows,
    asked, near, search, values, rcols, rmine,
    modes_out, resid_out, theta_out, stiff_out, mass_out,
    stage, halo, others, st_hi, st_lo, image, part, got, gram, gram_got, gram_full, terms, terms_got,
    halo_send, halo_recv, all_send, all_recv, sum_send, sum_recv,
    red_send, red_recv, bc_send, bc_recv, th_send, th_recv,
):
    blk, block, width = search.shape
    half = blk // 2
    wide = gram.shape[1]
    mc = rcols.shape[0]
    rows = blk * block
    span = rows // parts
    bspan = blk // parts
    extra = stage.shape[3] - width
    per = width // extra
    groups = half // (per + 1)
    gspan = groups // parts
    chunk = gram_got.shape[2]
    owners = wide // chunk
    w = lax.axis_index("wire")
    c = lax.axis_index("col")

    def on_wire(k):
        return lax.rem(w + k + nw, nw)

    def on_col(k):
        return lax.rem(c + k + nc, nc)

    barrier = pltpu.get_barrier_semaphore()

    @pl.loop(1, nw)
    def _(k):
        pl.semaphore_signal(barrier, inc=1, device_id={"wire": on_wire(k)}, device_id_type=MESH)

    for k in range(1, nc):
        pl.semaphore_signal(barrier, inc=1, device_id={"col": on_col(k)}, device_id_type=MESH)

    def fetch(t):
        @pl.loop(t * gspan, (t + 1) * gspan)
        def _(g):
            for d in range(4):
                last = search[asked[d, g * (per + 1) + per]]
                for m in range(per):
                    stage[d, g * per + m] = jnp.concatenate(
                        [search[asked[d, g * (per + 1) + m]], last[:, m * extra:(m + 1) * extra]], axis=1
                    )

    def fetched(d, g):
        tiles = [halo[d, g * per + m] for m in range(per)]
        return [tile[:, :width] for tile in tiles] + [
            jnp.concatenate([tile[:, width:] for tile in tiles], axis=1)
        ]

    def halo_copy(d, t):
        js = pl.ds(t * gspan * per, gspan * per)
        return remote(
            stage.at[d, js], halo.at[d, js], halo_send.at[d, t], halo_recv.at[d, t],
            {"wire": on_wire(-DISTANCES[d])},
        )

    sibling = c + 1 - 2 * lax.rem(c, 2)

    def all_copy(slot, way, t, device):
        view = others.at[slot, :, pl.ds(t * span, span)]
        return remote(view, view, all_send.at[way, t], all_recv.at[way, t], {"col": device})

    def to_sibling(t):
        return all_copy(c, 1, t, sibling)

    def across(k, t):
        return all_copy(c, k, t, on_col(k))

    def forward(k, t):
        return all_copy(on_col(-k), k + 1, t, sibling)

    def arrival(slot, way, t):
        return all_copy(slot, way, t, sibling)

    def sum_copy(k, t):
        ls = pl.ds(t * span, span)
        return remote(
            part.at[on_col(k), :, ls], got.at[k - 1, :, ls],
            sum_send.at[k - 1, t], sum_recv.at[k - 1, t], {"col": on_col(k)},
        )

    def red_copy(g, k):
        p = on_wire(k)
        first = pl.multiple_of(lax.rem(p, owners) * chunk, 8)
        return remote(
            gram.at[g, pl.ds(first, chunk)], gram_got.at[g, k],
            red_send.at[g, k], red_recv.at[g, k], {"wire": p},
        )

    def start_red(g):
        @pl.loop(1, nw)
        def _(k):
            if owners == nw:
                red_copy(g, k).start()
            else:
                @pl.when(on_wire(k) < owners)
                def _():
                    red_copy(g, k).start()

    def bc_copy(k, origin):
        first = pl.multiple_of(lax.rem(origin, owners) * chunk, 8)
        view = gram_full.at[:, pl.ds(first, chunk)]
        return remote(view, view, bc_send.at[k], bc_recv.at[k], {"wire": on_wire(k)})

    def th_copy(k):
        return remote(terms, terms_got.at[k], th_send.at[k], th_recv.at[k], {"wire": on_wire(k)})

    fetch(0)
    pl.semaphore_wait(barrier, nw + nc - 2)
    for t in range(parts):
        if t > 0:
            fetch(t)
        for d in (3, 1, 0, 2):
            halo_copy(d, t).start()
        others[c, :, t * span:(t + 1) * span] = search[t * bspan:(t + 1) * bspan].reshape(span, width).T
        for k in range(2, nc, 2):
            across(k, t).start()
        to_sibling(t).start()

    for t in range(parts):
        @pl.loop(t * bspan, (t + 1) * bspan)
        def _(i):
            mine = search[i]
            picked = jnp.concatenate([mine, search[near[i]]], axis=0)
            image[i] = 4.0 * mine + product(split(values[i][:, :2 * block]), split(picked))

        for k in range(2, nc, 2):
            arrival(on_col(-k), k, t).wait_recv()
            forward(k, t).start()

    rc = split(rcols[...])
    gram[...] = jnp.zeros_like(gram)

    for t in range(parts):
        ls = slice(t * span, (t + 1) * span)
        arrival(sibling, 1, t).wait_recv()
        for k in range(2, nc, 2):
            arrival(lax.rem(sibling - k + nc, nc), k + 1, t).wait_recv()
        for q in range(nc):
            high, low = split(others[q, :, ls])
            st_hi[q * width:(q + 1) * width, ls] = high
            st_lo[q * width:(q + 1) * width, ls] = low
        here = (st_hi[:, ls], st_lo[:, ls])
        own = split(search[t * bspan:(t + 1) * bspan].reshape(span, width))
        gram[1] += product(here, own)
        modes_out[:, ls] = product(rc, here)

    start_red(1)

    rm = split(rmine[...])
    for t in range(parts):
        for d in range(4):
            halo_copy(d, t).wait_recv()

        @pl.loop(t * gspan, (t + 1) * gspan)
        def _(g):
            for odd in range(2):
                pieces = zip(fetched(2 * odd, g), fetched(2 * odd + 1, g))
                for m, pair in enumerate(pieces):
                    i = 2 * (g * (per + 1) + m) + odd
                    picked = jnp.concatenate(pair, axis=0)
                    image[i] += product(split(values[i][:, 2 * block:]), split(picked))

        img = split(image[t * bspan:(t + 1) * bspan].reshape(span, width))
        turned = product(rm, img, NT)
        for q in range(nc):
            part[q, :, t * span:(t + 1) * span] = turned[q * mc:(q + 1) * mc]
        for k in range(1, nc):
            sum_copy(k, t).start()
        here = (st_hi[:, t * span:(t + 1) * span], st_lo[:, t * span:(t + 1) * span])
        gram[0] += product(here, img)

    start_red(0)

    numer = jnp.zeros((mc, 1), jnp.float32)
    denom = jnp.zeros((mc, 1), jnp.float32)
    for t in range(parts):
        ls = slice(t * span, (t + 1) * span)
        for k in range(1, nc):
            sum_copy(k, t).wait_recv()
        mine = part[c, :, ls]
        for k in range(1, nc):
            mine = mine + got[k - 1, :, ls]
        resid_out[:, ls] = mine
        modes = modes_out[:, ls]
        numer = numer + jnp.sum(modes * mine, axis=1, keepdims=True)
        denom = denom + jnp.sum(modes * modes, axis=1, keepdims=True)
    lane = lax.broadcasted_iota(jnp.int32, terms.shape, 1)
    terms[...] = jnp.where(lane < 64, numer, denom)

    @pl.loop(1, nw)
    def _(k):
        th_copy(k).start()

    def own_chunk():
        first = pl.multiple_of(lax.rem(w, owners) * chunk, 8)
        for g in range(2):
            gram_got[g, 0] = gram[g, pl.ds(first, chunk)]

            @pl.loop(1, nw)
            def _(k):
                red_copy(g, k).wait_recv()
                gram_got[g, 0] += gram_got[g, k]

            gram_full[g, pl.ds(first, chunk)] = gram_got[g, 0] * (1.0 / total_rows)

        @pl.loop(1, nw)
        def _(k):
            bc_copy(k, w).start()

    if owners == nw:
        own_chunk()
    else:
        pl.when(w < owners)(own_chunk)

    terms_got[0] = terms[...]

    @pl.loop(1, nw)
    def _(k):
        th_copy(k).wait_recv()
        terms_got[0] += terms_got[k]

    sums = terms_got[0]
    theta = sums[:, 0:1] / sums[:, 64:65]
    theta_out[...] = jnp.broadcast_to(theta, theta_out.shape)
    resid_out[...] = resid_out[...] - modes_out[...] * theta

    @pl.loop(1, nw)
    def _(k):
        th_copy(k).wait_send()
        if owners == nw:
            bc_copy(k, on_wire(-k)).wait_recv()
            bc_copy(k, w).wait_send()
            red_copy(0, k).wait_send()
            red_copy(1, k).wait_send()
        else:
            @pl.when(on_wire(-k) < owners)
            def _():
                bc_copy(k, on_wire(-k)).wait_recv()

            @pl.when(w < owners)
            def _():
                bc_copy(k, w).wait_send()

            @pl.when(on_wire(k) < owners)
            def _():
                red_copy(0, k).wait_send()
                red_copy(1, k).wait_send()

    stiff_out[...] = gram_full[0]
    mass_out[...] = gram_full[1]
    for t in range(parts):
        for d in range(4):
            halo_copy(d, t).wait_send()
        for k in range(1, nc):
            sum_copy(k, t).wait_send()
    for t in range(parts):
        to_sibling(t).wait_send()
        for k in range(2, nc, 2):
            across(k, t).wait_send()
            forward(k, t).wait_send()


def shards(search, block_values, block_cols, ritz):
    rows, width = search.shape
    blk, slots = block_cols.shape
    assert blk % 2 == 0 and slots == 4
    block = rows // blk
    half = blk // 2
    wide, modes = ritz.shape
    nw, nc = lax.axis_size("wire"), lax.axis_size("col")
    mc = modes // nc
    c = lax.axis_index("col")
    extra = -width % 128
    per = width // extra
    assert width % extra == 0 and half % (per + 1) == 0 and nc % 2 == 0
    groups = half // (per + 1)
    parts = next(n for n in (3, 2, 1) if groups % n == 0 and (rows // n) % 128 == 0)
    chunk = max(8, -(-wide // nw) // 8 * 8)
    assert wide % chunk == 0 and wide // chunk <= nw
    owners = wide // chunk
    local = block_cols % blk
    asked = []
    for distance, wanted in zip(
        DISTANCES, (local[0::2, 2], local[0::2, 3], local[1::2, 2], local[1::2, 3])
    ):
        asked.append(lax.ppermute(wanted, "wire", [(i, (i + distance) % nw) for i in range(nw)]))
    asked = jnp.stack(asked)
    rcols = lax.dynamic_slice_in_dim(ritz, c * mc, mc, 1).T
    rmine = lax.dynamic_slice_in_dim(ritz, c * width, width, 0).T
    f32 = jnp.float32
    vmem = pl.BlockSpec(memory_space=pltpu.VMEM)
    smem = pl.BlockSpec(memory_space=pltpu.SMEM)
    dma = pltpu.SemaphoreType.DMA
    modes_t, resid_t, theta, stiff, mass = pl.pallas_call(
        functools.partial(kernel, nw, nc, parts, float(rows * nw)),
        out_shape=(
            jax.ShapeDtypeStruct((mc, rows), f32),
            jax.ShapeDtypeStruct((mc, rows), f32),
            jax.ShapeDtypeStruct((mc, 128), f32),
            jax.ShapeDtypeStruct((wide, width), f32),
            jax.ShapeDtypeStruct((wide, width), f32),
        ),
        in_specs=[smem, smem, vmem, vmem, vmem, vmem],
        out_specs=(vmem,) * 5,
        scratch_shapes=[
            pltpu.VMEM((4, groups * per, block, width + extra), f32),
            pltpu.VMEM((4, groups * per, block, width + extra), f32),
            pltpu.VMEM((nc, width, rows), f32),
            pltpu.VMEM((wide, rows), jnp.bfloat16),
            pltpu.VMEM((wide, rows), jnp.bfloat16),
            pltpu.VMEM((blk, block, width), f32),
            pltpu.VMEM((nc, mc, rows), f32),
            pltpu.VMEM((nc - 1, mc, rows), f32),
            pltpu.VMEM((2, wide, width), f32),
            pltpu.VMEM((2, nw, chunk, width), f32),
            pltpu.VMEM((2, wide, width), f32),
            pltpu.VMEM((mc, 128), f32),
            pltpu.VMEM((nw, mc, 128), f32),
            dma((4, parts)), dma((4, parts)),
            dma((nc, parts)), dma((nc, parts)),
            dma((nc - 1, parts)), dma((nc - 1, parts)),
            dma((2, nw)), dma((2, nw)),
            dma((nw,)), dma((nw,)),
            dma((nw,)), dma((nw,)),
        ],
        compiler_params=pltpu.CompilerParams(
            collective_id=0, has_side_effects=True, vmem_limit_bytes=56 * 1024 * 1024
        ),
        name="step",
    )(asked, local[:, 1], search.reshape(blk, block, width),
      block_values.reshape(blk, block, slots * block), rcols, rmine)
    return modes_t.T, resid_t.T, theta[:, 0], stiff, mass


def solution(mesh):
    placed = (P("wire", "col"), P("wire", None), P("wire", None), P())
    return jax.shard_map(
        shards,
        mesh=mesh,
        in_specs=placed,
        out_specs=(P("wire", "col"), P("wire", "col"), P("col"), P(None, "col"), P(None, "col")),
        check_vma=False,
    )
```

```python
import functools

import jax
import jax.numpy as jnp
from jax import lax
from jax.experimental import pallas as pl
from jax.experimental.pallas import tpu as pltpu
from jax.sharding import PartitionSpec as P

MESH = pl.DeviceIdType.MESH
DISTANCES = (1, 2, -1, -2)
NN = (((1,), (0,)), ((), ()))
NT = (((1,), (1,)), ((), ()))


def split(x):
    high = x.astype(jnp.bfloat16)
    return high, (x - high.astype(jnp.float32)).astype(jnp.bfloat16)


def product(a, b, dims=NN):
    mul = functools.partial(lax.dot_general, dimension_numbers=dims, preferred_element_type=jnp.float32)
    return mul(a[0], b[0]) + (mul(a[0], b[1]) + mul(a[1], b[0]))


def remote(src, dst, send, recv, device):
    return pltpu.make_async_remote_copy(
        src_ref=src, dst_ref=dst, send_sem=send, recv_sem=recv, device_id=device, device_id_type=MESH
    )


def kernel(
    nw, nc, parts, total_rows,
    named, wanted, search_t, values, ritz,
    modes_out, resid_out, theta_out, stiff_out, mass_out,
    search, ritz_t, requests, asked, stage, halo, others, st_hi, st_lo, image, part, got, gram, gram_got, gram_full, terms, terms_got,
    ask_send, ask_recv, ask_local, halo_send, halo_recv, all_send, all_recv, sum_send, sum_recv,
    red_send, red_recv, bc_send, bc_recv, th_send, th_recv,
):
    blk, block, width = search.shape
    half = blk // 2
    wide = gram.shape[1]
    mc = modes_out.shape[0]
    rows = blk * block
    span = rows // parts
    bspan = blk // parts
    extra = stage.shape[3] - width
    per = width // extra
    groups = half // (per + 1)
    gspan = groups // parts
    chunk = gram_got.shape[2]
    owners = wide // chunk
    w = lax.axis_index("wire")
    c = lax.axis_index("col")

    def on_wire(k):
        return lax.rem(w + k + nw, nw)

    def on_col(k):
        return lax.rem(c + k + nc, nc)

    barrier = pltpu.get_barrier_semaphore()

    @pl.loop(1, nw)
    def _(k):
        pl.semaphore_signal(barrier, inc=1, device_id={"wire": on_wire(k)}, device_id_type=MESH)

    for k in range(1, nc):
        pl.semaphore_signal(barrier, inc=1, device_id={"col": on_col(k)}, device_id_type=MESH)

    def requested(d, j):
        return search[lax.rem(asked[d, 2 + d % 2, 2 * j + d // 2], blk)]

    def fetch(t):
        @pl.loop(t * gspan, (t + 1) * gspan)
        def _(g):
            for d in range(4):
                last = requested(d, g * (per + 1) + per)
                for m in range(per):
                    stage[d, g * per + m] = jnp.concatenate(
                        [requested(d, g * (per + 1) + m), last[:, m * extra:(m + 1) * extra]], axis=1
                    )

    def fetched(d, g):
        tiles = [halo[d, g * per + m] for m in range(per)]
        return [tile[:, :width] for tile in tiles] + [
            jnp.concatenate([tile[:, width:] for tile in tiles], axis=1)
        ]

    def ask_copy(d):
        return remote(
            wanted, requests.at[d], ask_send.at[d], ask_recv.at[d], {"wire": on_wire(DISTANCES[d])}
        )

    def halo_copy(d, t):
        js = pl.ds(t * gspan * per, gspan * per)
        return remote(
            stage.at[d, js], halo.at[d, js], halo_send.at[d, t], halo_recv.at[d, t],
            {"wire": on_wire(-DISTANCES[d])},
        )

    sibling = c + 1 - 2 * lax.rem(c, 2)

    def all_copy(slot, way, t, device, own=False):
        view = others.at[slot, :, pl.ds(t * span, span)]
        src = search_t.at[:, pl.ds(t * span, span)] if own else view
        return remote(src, view, all_send.at[way, t], all_recv.at[way, t], {"col": device})

    def to_sibling(t):
        return all_copy(c, 1, t, sibling, True)

    def across(k, t):
        return all_copy(c, k, t, on_col(k), True)

    def forward(k, t):
        return all_copy(on_col(-k), k + 1, t, sibling)

    def arrival(slot, way, t):
        return all_copy(slot, way, t, sibling)

    def sum_copy(k, t):
        ls = pl.ds(t * span, span)
        return remote(
            part.at[on_col(k), :, ls], got.at[k - 1, :, ls],
            sum_send.at[k - 1, t], sum_recv.at[k - 1, t], {"col": on_col(k)},
        )

    def red_copy(g, k):
        p = on_wire(k)
        first = pl.multiple_of(lax.rem(p, owners) * chunk, 8)
        return remote(
            gram.at[g, pl.ds(first, chunk)], gram_got.at[g, k],
            red_send.at[g, k], red_recv.at[g, k], {"wire": p},
        )

    def start_red(g):
        @pl.loop(1, nw)
        def _(k):
            if owners == nw:
                red_copy(g, k).start()
            else:
                @pl.when(on_wire(k) < owners)
                def _():
                    red_copy(g, k).start()

    def bc_copy(k, origin):
        first = pl.multiple_of(lax.rem(origin, owners) * chunk, 8)
        view = gram_full.at[:, pl.ds(first, chunk)]
        return remote(view, view, bc_send.at[k], bc_recv.at[k], {"wire": on_wire(k)})

    def th_copy(k):
        return remote(terms, terms_got.at[k], th_send.at[k], th_recv.at[k], {"wire": on_wire(k)})

    pl.semaphore_wait(barrier, nw + nc - 2)
    for d in range(4):
        ask_copy(d).start()
    for t in range(parts):
        for k in range(2, nc, 2):
            across(k, t).start()
        to_sibling(t).start()
    for t in range(parts):
        turned = search_t[:, t * span:(t + 1) * span].T
        search[t * bspan:(t + 1) * bspan] = turned.reshape(bspan, block, width)
    for d in range(4):
        ask_copy(d).wait_recv()
    down = pltpu.make_async_copy(requests, asked, ask_local)
    down.start()
    down.wait()
    for t in range(parts):
        fetch(t)
        for d in (3, 1, 0, 2):
            halo_copy(d, t).start()
    others[c] = search_t[...]
    ritz_t[...] = ritz[...].T

    for t in range(parts):
        @pl.loop(t * bspan, (t + 1) * bspan)
        def _(i):
            mine = search[i]
            picked = jnp.concatenate([mine, search[lax.rem(named[1, i], blk)]], axis=0)
            image[i] = 4.0 * mine + product(split(values[i][:, :2 * block]), split(picked))

        for k in range(2, nc, 2):
            arrival(on_col(-k), k, t).wait_recv()
            forward(k, t).start()

    rc = split(ritz_t[pl.ds(pl.multiple_of(c * mc, 8), mc)])
    gram[...] = jnp.zeros_like(gram)

    for t in range(parts):
        ls = slice(t * span, (t + 1) * span)
        arrival(sibling, 1, t).wait_recv()
        for k in range(2, nc, 2):
            arrival(lax.rem(sibling - k + nc, nc), k + 1, t).wait_recv()
        for q in range(nc):
            high, low = split(others[q, :, ls])
            st_hi[q * width:(q + 1) * width, ls] = high
            st_lo[q * width:(q + 1) * width, ls] = low
        here = (st_hi[:, ls], st_lo[:, ls])
        own = split(search[t * bspan:(t + 1) * bspan].reshape(span, width))
        gram[1] += product(here, own)
        modes_out[:, ls] = product(rc, here)

    start_red(1)

    rm = split(ritz[pl.ds(pl.multiple_of(c * width, 8), width)].T)
    for t in range(parts):
        for d in range(4):
            halo_copy(d, t).wait_recv()

        @pl.loop(t * gspan, (t + 1) * gspan)
        def _(g):
            for odd in range(2):
                pieces = zip(fetched(2 * odd, g), fetched(2 * odd + 1, g))
                for m, pair in enumerate(pieces):
                    i = 2 * (g * (per + 1) + m) + odd
                    picked = jnp.concatenate(pair, axis=0)
                    image[i] += product(split(values[i][:, 2 * block:]), split(picked))

        img = split(image[t * bspan:(t + 1) * bspan].reshape(span, width))
        turned = product(rm, img, NT)
        for q in range(nc):
            part[q, :, t * span:(t + 1) * span] = turned[q * mc:(q + 1) * mc]
        for k in range(1, nc):
            sum_copy(k, t).start()
        here = (st_hi[:, t * span:(t + 1) * span], st_lo[:, t * span:(t + 1) * span])
        gram[0] += product(here, img)

    start_red(0)

    numer = jnp.zeros((mc, 1), jnp.float32)
    denom = jnp.zeros((mc, 1), jnp.float32)
    for t in range(parts):
        ls = slice(t * span, (t + 1) * span)
        for k in range(1, nc):
            sum_copy(k, t).wait_recv()
        mine = part[c, :, ls]
        for k in range(1, nc):
            mine = mine + got[k - 1, :, ls]
        resid_out[:, ls] = mine
        modes = modes_out[:, ls]
        numer = numer + jnp.sum(modes * mine, axis=1, keepdims=True)
        denom = denom + jnp.sum(modes * modes, axis=1, keepdims=True)
    lane = lax.broadcasted_iota(jnp.int32, terms.shape, 1)
    terms[...] = jnp.where(lane < 64, numer, denom)

    @pl.loop(1, nw)
    def _(k):
        th_copy(k).start()

    def own_chunk():
        first = pl.multiple_of(lax.rem(w, owners) * chunk, 8)
        for g in range(2):
            gram_got[g, 0] = gram[g, pl.ds(first, chunk)]

            @pl.loop(1, nw)
            def _(k):
                red_copy(g, k).wait_recv()
                gram_got[g, 0] += gram_got[g, k]

            gram_full[g, pl.ds(first, chunk)] = gram_got[g, 0] * (1.0 / total_rows)

        @pl.loop(1, nw)
        def _(k):
            bc_copy(k, w).start()

    if owners == nw:
        own_chunk()
    else:
        pl.when(w < owners)(own_chunk)

    terms_got[0] = terms[...]

    @pl.loop(1, nw)
    def _(k):
        th_copy(k).wait_recv()
        terms_got[0] += terms_got[k]

    sums = terms_got[0]
    theta = sums[:, 0:1] / sums[:, 64:65]
    theta_out[...] = jnp.broadcast_to(theta, terms.shape).T[:theta_out.shape[0]]
    resid_out[...] = resid_out[...] - modes_out[...] * theta

    @pl.loop(1, nw)
    def _(k):
        th_copy(k).wait_send()
        if owners == nw:
            bc_copy(k, on_wire(-k)).wait_recv()
            bc_copy(k, w).wait_send()
            red_copy(0, k).wait_send()
            red_copy(1, k).wait_send()
        else:
            @pl.when(on_wire(-k) < owners)
            def _():
                bc_copy(k, on_wire(-k)).wait_recv()

            @pl.when(w < owners)
            def _():
                bc_copy(k, w).wait_send()

            @pl.when(on_wire(k) < owners)
            def _():
                red_copy(0, k).wait_send()
                red_copy(1, k).wait_send()

    stiff_out[...] = gram_full[0].T
    mass_out[...] = gram_full[1].T
    for d in range(4):
        ask_copy(d).wait_send()
    for t in range(parts):
        for d in range(4):
            halo_copy(d, t).wait_send()
        for k in range(1, nc):
            sum_copy(k, t).wait_send()
    for t in range(parts):
        to_sibling(t).wait_send()
        for k in range(2, nc, 2):
            across(k, t).wait_send()
            forward(k, t).wait_send()


def shards(search, block_values, block_cols, ritz):
    rows, width = search.shape
    blk, slots = block_cols.shape
    assert blk % 2 == 0 and slots == 4
    block = rows // blk
    half = blk // 2
    wide, modes = ritz.shape
    nw, nc = lax.axis_size("wire"), lax.axis_size("col")
    mc = modes // nc
    extra = -width % 128
    per = width // extra
    assert width % extra == 0 and half % (per + 1) == 0 and nc % 2 == 0
    groups = half // (per + 1)
    parts = next(n for n in (3, 2, 1) if groups % n == 0 and (rows // n) % 128 == 0)
    chunk = max(8, -(-wide // nw) // 8 * 8)
    assert wide % chunk == 0 and wide // chunk <= nw
    owners = wide // chunk
    wanted = jnp.pad(block_cols.T, ((0, -slots % 8), (0, -blk % 128)))
    f32 = jnp.float32
    vmem = pl.BlockSpec(memory_space=pltpu.VMEM)
    smem = pl.BlockSpec(memory_space=pltpu.SMEM)
    dma = pltpu.SemaphoreType.DMA
    modes_t, resid_t, theta, stiff, mass = pl.pallas_call(
        functools.partial(kernel, nw, nc, parts, float(rows * nw)),
        out_shape=(
            jax.ShapeDtypeStruct((mc, rows), f32),
            jax.ShapeDtypeStruct((mc, rows), f32),
            jax.ShapeDtypeStruct((8, mc), f32),
            jax.ShapeDtypeStruct((width, wide), f32),
            jax.ShapeDtypeStruct((width, wide), f32),
        ),
        in_specs=[smem, vmem, vmem, vmem, vmem],
        out_specs=(vmem,) * 5,
        scratch_shapes=[
            pltpu.VMEM((blk, block, width), f32),
            pltpu.VMEM((modes, wide), f32),
            pltpu.VMEM((4, *wanted.shape), jnp.int32),
            pltpu.SMEM((4, *wanted.shape), jnp.int32),
            pltpu.VMEM((4, groups * per, block, width + extra), f32),
            pltpu.VMEM((4, groups * per, block, width + extra), f32),
            pltpu.VMEM((nc, width, rows), f32),
            pltpu.VMEM((wide, rows), jnp.bfloat16),
            pltpu.VMEM((wide, rows), jnp.bfloat16),
            pltpu.VMEM((blk, block, width), f32),
            pltpu.VMEM((nc, mc, rows), f32),
            pltpu.VMEM((nc - 1, mc, rows), f32),
            pltpu.VMEM((2, wide, width), f32),
            pltpu.VMEM((2, nw, chunk, width), f32),
            pltpu.VMEM((2, wide, width), f32),
            pltpu.VMEM((mc, 128), f32),
            pltpu.VMEM((nw, mc, 128), f32),
            dma((4,)), dma((4,)), dma,
            dma((4, parts)), dma((4, parts)),
            dma((nc, parts)), dma((nc, parts)),
            dma((nc - 1, parts)), dma((nc - 1, parts)),
            dma((2, nw)), dma((2, nw)),
            dma((nw,)), dma((nw,)),
            dma((nw,)), dma((nw,)),
        ],
        compiler_params=pltpu.CompilerParams(
            collective_id=0, has_side_effects=True, vmem_limit_bytes=56 * 1024 * 1024
        ),
        name="step",
    )(wanted, wanted, search.T, block_values.reshape(blk, block, slots * block), ritz)
    return modes_t.T, resid_t.T, theta[0], stiff.T, mass.T


def solution(mesh):
    placed = (P("wire", "col"), P("wire", None), P("wire", None), P())
    return jax.shard_map(
        shards,
        mesh=mesh,
        in_specs=placed,
        out_specs=(P("wire", "col"), P("wire", "col"), P("col"), P(None, "col"), P(None, "col")),
        check_vma=False,
    )
```

```python
import functools

import jax
import jax.numpy as jnp
from jax import lax
from jax.experimental import pallas as pl
from jax.experimental.pallas import tpu as pltpu
from jax.sharding import PartitionSpec as P

MESH = pl.DeviceIdType.MESH
DISTANCES = (1, 2, -1, -2)
NN = (((1,), (0,)), ((), ()))
NT = (((1,), (1,)), ((), ()))


def split(x):
    high = x.astype(jnp.bfloat16)
    return high, (x - high.astype(jnp.float32)).astype(jnp.bfloat16)


def product(a, b, dims=NN):
    mul = functools.partial(lax.dot_general, dimension_numbers=dims, preferred_element_type=jnp.float32)
    return mul(a[0], b[0]) + (mul(a[0], b[1]) + mul(a[1], b[0]))


def remote(src, dst, send, recv, device):
    return pltpu.make_async_remote_copy(
        src_ref=src, dst_ref=dst, send_sem=send, recv_sem=recv, device_id=device, device_id_type=MESH
    )


def kernel(
    nw, nc, parts, total_rows,
    named, wanted, search_t, values, ritz,
    modes_out, image_out, theta_out, stiff_out, mass_out,
    search, ritz_t, requests, asked, stage, halo, others, st_hi, st_lo, image, part, got, gram, gram_got, gram_full, terms, terms_got,
    ask_send, ask_recv, ask_local, halo_send, halo_recv, all_send, all_recv, sum_send, sum_recv,
    red_send, red_recv, bc_send, bc_recv, th_send, th_recv,
):
    blk, block, width = search.shape
    half = blk // 2
    wide = gram.shape[1]
    mc = modes_out.shape[0]
    rows = blk * block
    span = rows // parts
    bspan = blk // parts
    extra = stage.shape[3] - width
    per = width // extra
    groups = half // (per + 1)
    gspan = groups // parts
    chunk = gram_got.shape[2]
    owners = wide // chunk
    w = lax.axis_index("wire")
    c = lax.axis_index("col")

    def on_wire(k):
        return lax.rem(w + k + nw, nw)

    def on_col(k):
        return lax.rem(c + k + nc, nc)

    barrier = pltpu.get_barrier_semaphore()

    @pl.loop(1, nw)
    def _(k):
        pl.semaphore_signal(barrier, inc=1, device_id={"wire": on_wire(k)}, device_id_type=MESH)

    for k in range(1, nc):
        pl.semaphore_signal(barrier, inc=1, device_id={"col": on_col(k)}, device_id_type=MESH)

    def requested(d, j):
        return search[lax.rem(asked[d, 2 + d % 2, 2 * j + d // 2], blk)]

    def fetch(t):
        @pl.loop(t * gspan, (t + 1) * gspan)
        def _(g):
            for d in range(4):
                last = requested(d, g * (per + 1) + per)
                for m in range(per):
                    stage[d, g * per + m] = jnp.concatenate(
                        [requested(d, g * (per + 1) + m), last[:, m * extra:(m + 1) * extra]], axis=1
                    )

    def fetched(d, g):
        tiles = [halo[d, g * per + m] for m in range(per)]
        return [tile[:, :width] for tile in tiles] + [
            jnp.concatenate([tile[:, width:] for tile in tiles], axis=1)
        ]

    def ask_copy(d):
        return remote(
            wanted, requests.at[d], ask_send.at[d], ask_recv.at[d], {"wire": on_wire(DISTANCES[d])}
        )

    def halo_copy(d, t):
        js = pl.ds(t * gspan * per, gspan * per)
        return remote(
            stage.at[d, js], halo.at[d, js], halo_send.at[d, t], halo_recv.at[d, t],
            {"wire": on_wire(-DISTANCES[d])},
        )

    sibling = c + 1 - 2 * lax.rem(c, 2)

    def all_copy(slot, way, t, device, own=False):
        view = others.at[slot, :, pl.ds(t * span, span)]
        src = search_t.at[:, pl.ds(t * span, span)] if own else view
        return remote(src, view, all_send.at[way, t], all_recv.at[way, t], {"col": device})

    def to_sibling(t):
        return all_copy(c, 1, t, sibling, True)

    def across(k, t):
        return all_copy(c, k, t, on_col(k), True)

    def forward(k, t):
        return all_copy(on_col(-k), k + 1, t, sibling)

    def arrival(slot, way, t):
        return all_copy(slot, way, t, sibling)

    def sum_copy(k, t):
        ls = pl.ds(t * span, span)
        return remote(
            part.at[on_col(k), :, ls], got.at[k - 1, :, ls],
            sum_send.at[k - 1, t], sum_recv.at[k - 1, t], {"col": on_col(k)},
        )

    def red_copy(g, k):
        p = on_wire(k)
        first = pl.multiple_of(lax.rem(p, owners) * chunk, 8)
        return remote(
            gram.at[g, pl.ds(first, chunk)], gram_got.at[g, k],
            red_send.at[g, k], red_recv.at[g, k], {"wire": p},
        )

    def start_red(g):
        @pl.loop(1, nw)
        def _(k):
            if owners == nw:
                red_copy(g, k).start()
            else:
                @pl.when(on_wire(k) < owners)
                def _():
                    red_copy(g, k).start()

    def bc_copy(k, origin):
        first = pl.multiple_of(lax.rem(origin, owners) * chunk, 8)
        view = gram_full.at[:, pl.ds(first, chunk)]
        return remote(view, view, bc_send.at[k], bc_recv.at[k], {"wire": on_wire(k)})

    def th_copy(k):
        return remote(terms, terms_got.at[k], th_send.at[k], th_recv.at[k], {"wire": on_wire(k)})

    pl.semaphore_wait(barrier, nw + nc - 2)
    for d in range(4):
        ask_copy(d).start()
    for t in range(parts):
        for k in range(2, nc, 2):
            across(k, t).start()
        to_sibling(t).start()
    for t in range(parts):
        turned = search_t[:, t * span:(t + 1) * span].T
        search[t * bspan:(t + 1) * bspan] = turned.reshape(bspan, block, width)
    for d in range(4):
        ask_copy(d).wait_recv()
    down = pltpu.make_async_copy(requests, asked, ask_local)
    down.start()
    down.wait()
    for t in range(parts):
        fetch(t)
        for d in (3, 1, 0, 2):
            halo_copy(d, t).start()
    others[c] = search_t[...]
    ritz_t[...] = ritz[...].T

    for t in range(parts):
        @pl.loop(t * bspan, (t + 1) * bspan)
        def _(i):
            mine = search[i]
            picked = jnp.concatenate([mine, search[lax.rem(named[1, i], blk)]], axis=0)
            image[i] = 4.0 * mine + product(split(values[i][:, :2 * block]), split(picked))

        for k in range(2, nc, 2):
            arrival(on_col(-k), k, t).wait_recv()
            forward(k, t).start()

    rc = split(ritz_t[pl.ds(pl.multiple_of(c * mc, 8), mc)])
    gram[...] = jnp.zeros_like(gram)

    for t in range(parts):
        ls = slice(t * span, (t + 1) * span)
        arrival(sibling, 1, t).wait_recv()
        for k in range(2, nc, 2):
            arrival(lax.rem(sibling - k + nc, nc), k + 1, t).wait_recv()
        for q in range(nc):
            high, low = split(others[q, :, ls])
            st_hi[q * width:(q + 1) * width, ls] = high
            st_lo[q * width:(q + 1) * width, ls] = low
        here = (st_hi[:, ls], st_lo[:, ls])
        own = split(search[t * bspan:(t + 1) * bspan].reshape(span, width))
        gram[1] += product(here, own)
        modes_out[:, ls] = product(rc, here)

    start_red(1)

    rm = split(ritz[pl.ds(pl.multiple_of(c * width, 8), width)].T)
    for t in range(parts):
        for d in range(4):
            halo_copy(d, t).wait_recv()

        @pl.loop(t * gspan, (t + 1) * gspan)
        def _(g):
            for odd in range(2):
                pieces = zip(fetched(2 * odd, g), fetched(2 * odd + 1, g))
                for m, pair in enumerate(pieces):
                    i = 2 * (g * (per + 1) + m) + odd
                    picked = jnp.concatenate(pair, axis=0)
                    image[i] += product(split(values[i][:, 2 * block:]), split(picked))

        img = split(image[t * bspan:(t + 1) * bspan].reshape(span, width))
        turned = product(rm, img, NT)
        for q in range(nc):
            part[q, :, t * span:(t + 1) * span] = turned[q * mc:(q + 1) * mc]
        for k in range(1, nc):
            sum_copy(k, t).start()
        here = (st_hi[:, t * span:(t + 1) * span], st_lo[:, t * span:(t + 1) * span])
        gram[0] += product(here, img)

    start_red(0)

    numer = jnp.zeros((mc, 1), jnp.float32)
    denom = jnp.zeros((mc, 1), jnp.float32)
    for t in range(parts):
        ls = slice(t * span, (t + 1) * span)
        for k in range(1, nc):
            sum_copy(k, t).wait_recv()
        mine = part[c, :, ls]
        for k in range(1, nc):
            mine = mine + got[k - 1, :, ls]
        image_out[:, ls] = mine
        modes = modes_out[:, ls]
        numer = numer + jnp.sum(modes * mine, axis=1, keepdims=True)
        denom = denom + jnp.sum(modes * modes, axis=1, keepdims=True)
    lane = lax.broadcasted_iota(jnp.int32, terms.shape, 1)
    terms[...] = jnp.where(lane < 64, numer, denom)

    @pl.loop(1, nw)
    def _(k):
        th_copy(k).start()

    def own_chunk():
        first = pl.multiple_of(lax.rem(w, owners) * chunk, 8)
        for g in range(2):
            gram_got[g, 0] = gram[g, pl.ds(first, chunk)]

            @pl.loop(1, nw)
            def _(k):
                red_copy(g, k).wait_recv()
                gram_got[g, 0] += gram_got[g, k]

            gram_full[g, pl.ds(first, chunk)] = gram_got[g, 0] * (1.0 / total_rows)

        @pl.loop(1, nw)
        def _(k):
            bc_copy(k, w).start()

    if owners == nw:
        own_chunk()
    else:
        pl.when(w < owners)(own_chunk)

    terms_got[0] = terms[...]

    @pl.loop(1, nw)
    def _(k):
        th_copy(k).wait_recv()
        terms_got[0] += terms_got[k]

    sums = terms_got[0]
    theta = sums[:, 0:1] / sums[:, 64:65]
    theta_out[...] = jnp.broadcast_to(theta, terms.shape)

    @pl.loop(1, nw)
    def _(k):
        th_copy(k).wait_send()
        if owners == nw:
            bc_copy(k, on_wire(-k)).wait_recv()
            bc_copy(k, w).wait_send()
            red_copy(0, k).wait_send()
            red_copy(1, k).wait_send()
        else:
            @pl.when(on_wire(-k) < owners)
            def _():
                bc_copy(k, on_wire(-k)).wait_recv()

            @pl.when(w < owners)
            def _():
                bc_copy(k, w).wait_send()

            @pl.when(on_wire(k) < owners)
            def _():
                red_copy(0, k).wait_send()
                red_copy(1, k).wait_send()

    stiff_out[...] = gram_full[0].T
    mass_out[...] = gram_full[1].T
    for d in range(4):
        ask_copy(d).wait_send()
    for t in range(parts):
        for d in range(4):
            halo_copy(d, t).wait_send()
        for k in range(1, nc):
            sum_copy(k, t).wait_send()
    for t in range(parts):
        to_sibling(t).wait_send()
        for k in range(2, nc, 2):
            across(k, t).wait_send()
            forward(k, t).wait_send()


def finish(modes, image, theta, stiff, mass, modes_out, resid_out, theta_out, stiff_out, mass_out):
    modes_out[...] = modes[...]
    resid_out[...] = image[...] - modes[...] * theta[:, 0:1]
    theta_out[...] = theta[...].T[0]
    stiff_out[...] = stiff[...]
    mass_out[...] = mass[...]


def shards(search, block_values, block_cols, ritz):
    rows, width = search.shape
    blk, slots = block_cols.shape
    assert blk % 2 == 0 and slots == 4
    block = rows // blk
    half = blk // 2
    wide, modes = ritz.shape
    nw, nc = lax.axis_size("wire"), lax.axis_size("col")
    mc = modes // nc
    extra = -width % 128
    per = width // extra
    assert width % extra == 0 and half % (per + 1) == 0 and nc % 2 == 0
    groups = half // (per + 1)
    parts = next(n for n in (6, 3, 2, 1) if groups % n == 0 and (rows // n) % 128 == 0)
    chunk = max(8, -(-wide // nw) // 8 * 8)
    assert wide % chunk == 0 and wide // chunk <= nw
    owners = wide // chunk
    wanted = jnp.pad(block_cols.T, ((0, -slots % 8), (0, -blk % 128)))
    f32 = jnp.float32
    vmem = pl.BlockSpec(memory_space=pltpu.VMEM)
    smem = pl.BlockSpec(memory_space=pltpu.SMEM)
    dma = pltpu.SemaphoreType.DMA
    results = pl.pallas_call(
        functools.partial(kernel, nw, nc, parts, float(rows * nw)),
        out_shape=(
            jax.ShapeDtypeStruct((mc, rows), f32),
            jax.ShapeDtypeStruct((mc, rows), f32),
            jax.ShapeDtypeStruct((mc, 128), f32),
            jax.ShapeDtypeStruct((width, wide), f32),
            jax.ShapeDtypeStruct((width, wide), f32),
        ),
        in_specs=[smem, vmem, vmem, vmem, vmem],
        out_specs=(vmem,) * 5,
        scratch_shapes=[
            pltpu.VMEM((blk, block, width), f32),
            pltpu.VMEM((modes, wide), f32),
            pltpu.VMEM((4, *wanted.shape), jnp.int32),
            pltpu.SMEM((4, *wanted.shape), jnp.int32),
            pltpu.VMEM((4, groups * per, block, width + extra), f32),
            pltpu.VMEM((4, groups * per, block, width + extra), f32),
            pltpu.VMEM((nc, width, rows), f32),
            pltpu.VMEM((wide, rows), jnp.bfloat16),
            pltpu.VMEM((wide, rows), jnp.bfloat16),
            pltpu.VMEM((blk, block, width), f32),
            pltpu.VMEM((nc, mc, rows), f32),
            pltpu.VMEM((nc - 1, mc, rows), f32),
            pltpu.VMEM((2, wide, width), f32),
            pltpu.VMEM((2, nw, chunk, width), f32),
            pltpu.VMEM((2, wide, width), f32),
            pltpu.VMEM((mc, 128), f32),
            pltpu.VMEM((nw, mc, 128), f32),
            dma((4,)), dma((4,)), dma,
            dma((4, parts)), dma((4, parts)),
            dma((nc, parts)), dma((nc, parts)),
            dma((nc - 1, parts)), dma((nc - 1, parts)),
            dma((2, nw)), dma((2, nw)),
            dma((nw,)), dma((nw,)),
            dma((nw,)), dma((nw,)),
        ],
        compiler_params=pltpu.CompilerParams(
            collective_id=0, has_side_effects=True, vmem_limit_bytes=56 * 1024 * 1024
        ),
        name="step",
    )(wanted, wanted, search.T, block_values.reshape(blk, block, slots * block), ritz)
    modes_t, resid_t, theta, stiff, mass = pl.pallas_call(
        finish,
        out_shape=tuple(
            jax.ShapeDtypeStruct(shape, f32)
            for shape in ((mc, rows), (mc, rows), (mc,), (width, wide), (width, wide))
        ),
        in_specs=[vmem] * 5,
        out_specs=(vmem,) * 5,
        compiler_params=pltpu.CompilerParams(vmem_limit_bytes=16 * 1024 * 1024),
        name="finish",
    )(*results)
    return modes_t.T, resid_t.T, theta, stiff.T, mass.T


def solution(mesh):
    placed = (P("wire", "col"), P("wire", None), P("wire", None), P())
    return jax.shard_map(
        shards,
        mesh=mesh,
        in_specs=placed,
        out_specs=(P("wire", "col"), P("wire", "col"), P("col"), P(None, "col"), P(None, "col")),
        check_vma=False,
    )
```

```python
import functools

import jax
import jax.numpy as jnp
from jax import lax
from jax.experimental import pallas as pl
from jax.experimental.pallas import tpu as pltpu
from jax.sharding import PartitionSpec as P

MESH = pl.DeviceIdType.MESH
DISTANCES = (1, 2, -1, -2)
NN = (((1,), (0,)), ((), ()))
NT = (((1,), (1,)), ((), ()))


def split(x):
    high = x.astype(jnp.bfloat16)
    return high, (x - high.astype(jnp.float32)).astype(jnp.bfloat16)


def product(a, b, dims=NN):
    mul = functools.partial(lax.dot_general, dimension_numbers=dims, preferred_element_type=jnp.float32)
    return mul(a[0], b[0]) + (mul(a[0], b[1]) + mul(a[1], b[0]))


def stacked(a, b):
    mul = functools.partial(jnp.dot, preferred_element_type=jnp.float32)
    rows = a[0].shape[0]
    both = mul(jnp.concatenate(a, axis=0), b[0])
    return both[:rows] + (both[rows:] + mul(a[0], b[1]))


def remote(src, dst, send, recv, device):
    return pltpu.make_async_remote_copy(
        src_ref=src, dst_ref=dst, send_sem=send, recv_sem=recv, device_id=device, device_id_type=MESH
    )


def kernel(
    nw, nc, parts, total_rows,
    named, wanted, search_t, values, ritz,
    modes_out, image_out, theta_out, stiff_out, mass_out,
    search, ritz_t, requests, asked, stage, halo, others, st_hi, st_lo, image, part, got, gram, gram_got, gram_full, terms, terms_got,
    ask_send, ask_recv, ask_local, halo_send, halo_recv, all_send, all_recv, sum_send, sum_recv,
    red_send, red_recv, bc_send, bc_recv, th_send, th_recv,
):
    blk, block, width = search.shape
    half = blk // 2
    wide = gram.shape[1]
    mc = modes_out.shape[0]
    rows = blk * block
    span = rows // parts
    bspan = blk // parts
    extra = stage.shape[3] - width
    per = width // extra
    groups = half // (per + 1)
    gspan = groups // parts
    chunk = gram_got.shape[2]
    owners = wide // chunk
    w = lax.axis_index("wire")
    c = lax.axis_index("col")

    def on_wire(k):
        return lax.rem(w + k + nw, nw)

    def on_col(k):
        return lax.rem(c + k + nc, nc)

    barrier = pltpu.get_barrier_semaphore()

    @pl.loop(1, nw)
    def _(k):
        pl.semaphore_signal(barrier, inc=1, device_id={"wire": on_wire(k)}, device_id_type=MESH)

    for k in range(1, nc):
        pl.semaphore_signal(barrier, inc=1, device_id={"col": on_col(k)}, device_id_type=MESH)

    def requested(d, j):
        return search[lax.rem(asked[d, 2 + d % 2, 2 * j + d // 2], blk)]

    def fetch(t):
        @pl.loop(t * gspan, (t + 1) * gspan)
        def _(g):
            for d in range(4):
                last = requested(d, g * (per + 1) + per)
                for m in range(per):
                    stage[d, g * per + m] = jnp.concatenate(
                        [requested(d, g * (per + 1) + m), last[:, m * extra:(m + 1) * extra]], axis=1
                    )

    def fetched(d, g):
        tiles = [halo[d, g * per + m] for m in range(per)]
        return [tile[:, :width] for tile in tiles] + [
            jnp.concatenate([tile[:, width:] for tile in tiles], axis=1)
        ]

    def ask_copy(d):
        return remote(
            wanted, requests.at[d], ask_send.at[d], ask_recv.at[d], {"wire": on_wire(DISTANCES[d])}
        )

    def halo_copy(d, t):
        js = pl.ds(t * gspan * per, gspan * per)
        return remote(
            stage.at[d, js], halo.at[d, js], halo_send.at[d, t], halo_recv.at[d, t],
            {"wire": on_wire(-DISTANCES[d])},
        )

    sibling = c + 1 - 2 * lax.rem(c, 2)

    def all_copy(slot, way, t, device, own=False):
        view = others.at[slot, :, pl.ds(t * span, span)]
        src = search_t.at[:, pl.ds(t * span, span)] if own else view
        return remote(src, view, all_send.at[way, t], all_recv.at[way, t], {"col": device})

    def to_sibling(t):
        return all_copy(c, 1, t, sibling, True)

    def across(k, t):
        return all_copy(c, k, t, on_col(k), True)

    def forward(k, t):
        return all_copy(on_col(-k), k + 1, t, sibling)

    def arrival(slot, way, t):
        return all_copy(slot, way, t, sibling)

    def sum_copy(k, t):
        ls = pl.ds(t * span, span)
        return remote(
            part.at[on_col(k), :, ls], got.at[k - 1, :, ls],
            sum_send.at[k - 1, t], sum_recv.at[k - 1, t], {"col": on_col(k)},
        )

    def red_copy(g, k):
        p = on_wire(k)
        first = pl.multiple_of(lax.rem(p, owners) * chunk, 8)
        return remote(
            gram.at[g, pl.ds(first, chunk)], gram_got.at[g, k],
            red_send.at[g, k], red_recv.at[g, k], {"wire": p},
        )

    def start_red(g):
        @pl.loop(1, nw)
        def _(k):
            if owners == nw:
                red_copy(g, k).start()
            else:
                @pl.when(on_wire(k) < owners)
                def _():
                    red_copy(g, k).start()

    def bc_copy(k, origin):
        first = pl.multiple_of(lax.rem(origin, owners) * chunk, 8)
        view = gram_full.at[:, pl.ds(first, chunk)]
        return remote(view, view, bc_send.at[k], bc_recv.at[k], {"wire": on_wire(k)})

    def th_copy(k):
        return remote(terms, terms_got.at[k], th_send.at[k], th_recv.at[k], {"wire": on_wire(k)})

    pl.semaphore_wait(barrier, nw + nc - 2)
    for d in range(4):
        ask_copy(d).start()
    for t in range(parts):
        for k in range(2, nc, 2):
            across(k, t).start()
        to_sibling(t).start()
    for t in range(parts):
        turned = search_t[:, t * span:(t + 1) * span].T
        search[t * bspan:(t + 1) * bspan] = turned.reshape(bspan, block, width)
    for d in range(4):
        ask_copy(d).wait_recv()
    down = pltpu.make_async_copy(requests, asked, ask_local)
    down.start()
    down.wait()
    for t in range(parts):
        fetch(t)
        for d in (3, 1, 0, 2):
            halo_copy(d, t).start()
    others[c] = search_t[...]
    ritz_t[...] = ritz[...].T

    for t in range(parts):
        @pl.loop(t * bspan, (t + 1) * bspan)
        def _(i):
            mine = search[i]
            picked = jnp.concatenate([mine, search[lax.rem(named[1, i], blk)]], axis=0)
            image[i] = 4.0 * mine + stacked(split(values[i][:, :2 * block]), split(picked))

        for k in range(2, nc, 2):
            arrival(on_col(-k), k, t).wait_recv()
            forward(k, t).start()

    rc = split(ritz_t[pl.ds(pl.multiple_of(c * mc, 8), mc)])
    gram[...] = jnp.zeros_like(gram)

    for t in range(parts):
        ls = slice(t * span, (t + 1) * span)
        arrival(sibling, 1, t).wait_recv()
        for k in range(2, nc, 2):
            arrival(lax.rem(sibling - k + nc, nc), k + 1, t).wait_recv()
        for q in range(nc):
            high, low = split(others[q, :, ls])
            st_hi[q * width:(q + 1) * width, ls] = high
            st_lo[q * width:(q + 1) * width, ls] = low
        here = (st_hi[:, ls], st_lo[:, ls])
        own = split(search[t * bspan:(t + 1) * bspan].reshape(span, width))
        gram[1] += product(here, own)
        modes_out[:, ls] = product(rc, here)

    start_red(1)

    rm = split(ritz[pl.ds(pl.multiple_of(c * width, 8), width)].T)
    for t in range(parts):
        for d in range(4):
            halo_copy(d, t).wait_recv()

        @pl.loop(t * gspan, (t + 1) * gspan)
        def _(g):
            for odd in range(2):
                pieces = zip(fetched(2 * odd, g), fetched(2 * odd + 1, g))
                for m, pair in enumerate(pieces):
                    i = 2 * (g * (per + 1) + m) + odd
                    picked = jnp.concatenate(pair, axis=0)
                    image[i] += stacked(split(values[i][:, 2 * block:]), split(picked))

        img = split(image[t * bspan:(t + 1) * bspan].reshape(span, width))
        turned = product(rm, img, NT)
        for q in range(nc):
            part[q, :, t * span:(t + 1) * span] = turned[q * mc:(q + 1) * mc]
        for k in range(1, nc):
            sum_copy(k, t).start()
        here = (st_hi[:, t * span:(t + 1) * span], st_lo[:, t * span:(t + 1) * span])
        gram[0] += product(here, img)

    start_red(0)

    numer = jnp.zeros((mc, 1), jnp.float32)
    denom = jnp.zeros((mc, 1), jnp.float32)
    for t in range(parts):
        ls = slice(t * span, (t + 1) * span)
        for k in range(1, nc):
            sum_copy(k, t).wait_recv()
        mine = part[c, :, ls]
        for k in range(1, nc):
            mine = mine + got[k - 1, :, ls]
        image_out[:, ls] = mine
        modes = modes_out[:, ls]
        numer = numer + jnp.sum(modes * mine, axis=1, keepdims=True)
        denom = denom + jnp.sum(modes * modes, axis=1, keepdims=True)
    lane = lax.broadcasted_iota(jnp.int32, terms.shape, 1)
    terms[...] = jnp.where(lane < 64, numer, denom)

    @pl.loop(1, nw)
    def _(k):
        th_copy(k).start()

    def own_chunk():
        first = pl.multiple_of(lax.rem(w, owners) * chunk, 8)
        for g in range(2):
            gram_got[g, 0] = gram[g, pl.ds(first, chunk)]

            @pl.loop(1, nw)
            def _(k):
                red_copy(g, k).wait_recv()
                gram_got[g, 0] += gram_got[g, k]

            gram_full[g, pl.ds(first, chunk)] = gram_got[g, 0] * (1.0 / total_rows)

        @pl.loop(1, nw)
        def _(k):
            bc_copy(k, w).start()

    if owners == nw:
        own_chunk()
    else:
        pl.when(w < owners)(own_chunk)

    terms_got[0] = terms[...]

    @pl.loop(1, nw)
    def _(k):
        th_copy(k).wait_recv()
        terms_got[0] += terms_got[k]

    sums = terms_got[0]
    theta = sums[:, 0:1] / sums[:, 64:65]
    theta_out[...] = jnp.broadcast_to(theta, terms.shape)

    @pl.loop(1, nw)
    def _(k):
        th_copy(k).wait_send()
        if owners == nw:
            bc_copy(k, on_wire(-k)).wait_recv()
            bc_copy(k, w).wait_send()
            red_copy(0, k).wait_send()
            red_copy(1, k).wait_send()
        else:
            @pl.when(on_wire(-k) < owners)
            def _():
                bc_copy(k, on_wire(-k)).wait_recv()

            @pl.when(w < owners)
            def _():
                bc_copy(k, w).wait_send()

            @pl.when(on_wire(k) < owners)
            def _():
                red_copy(0, k).wait_send()
                red_copy(1, k).wait_send()

    stiff_out[...] = gram_full[0].T
    mass_out[...] = gram_full[1].T
    for d in range(4):
        ask_copy(d).wait_send()
    for t in range(parts):
        for d in range(4):
            halo_copy(d, t).wait_send()
        for k in range(1, nc):
            sum_copy(k, t).wait_send()
    for t in range(parts):
        to_sibling(t).wait_send()
        for k in range(2, nc, 2):
            across(k, t).wait_send()
            forward(k, t).wait_send()


def finish(modes, image, theta, stiff, mass, modes_out, resid_out, theta_out, stiff_out, mass_out):
    modes_out[...] = modes[...]
    resid_out[...] = image[...] - modes[...] * theta[:, 0:1]
    theta_out[...] = theta[...].T[0]
    stiff_out[...] = stiff[...]
    mass_out[...] = mass[...]


def shards(search, block_values, block_cols, ritz):
    rows, width = search.shape
    blk, slots = block_cols.shape
    assert blk % 2 == 0 and slots == 4
    block = rows // blk
    half = blk // 2
    wide, modes = ritz.shape
    nw, nc = lax.axis_size("wire"), lax.axis_size("col")
    mc = modes // nc
    extra = -width % 128
    per = width // extra
    assert width % extra == 0 and half % (per + 1) == 0 and nc % 2 == 0
    groups = half // (per + 1)
    parts = next(n for n in (6, 3, 2, 1) if groups % n == 0 and (rows // n) % 128 == 0)
    chunk = max(8, -(-wide // nw) // 8 * 8)
    assert wide % chunk == 0 and wide // chunk <= nw
    owners = wide // chunk
    wanted = jnp.pad(block_cols.T, ((0, -slots % 8), (0, -blk % 128)))
    f32 = jnp.float32
    vmem = pl.BlockSpec(memory_space=pltpu.VMEM)
    smem = pl.BlockSpec(memory_space=pltpu.SMEM)
    dma = pltpu.SemaphoreType.DMA
    results = pl.pallas_call(
        functools.partial(kernel, nw, nc, parts, float(rows * nw)),
        out_shape=(
            jax.ShapeDtypeStruct((mc, rows), f32),
            jax.ShapeDtypeStruct((mc, rows), f32),
            jax.ShapeDtypeStruct((mc, 128), f32),
            jax.ShapeDtypeStruct((width, wide), f32),
            jax.ShapeDtypeStruct((width, wide), f32),
        ),
        in_specs=[smem, vmem, vmem, vmem, vmem],
        out_specs=(vmem,) * 5,
        scratch_shapes=[
            pltpu.VMEM((blk, block, width), f32),
            pltpu.VMEM((modes, wide), f32),
            pltpu.VMEM((4, *wanted.shape), jnp.int32),
            pltpu.SMEM((4, *wanted.shape), jnp.int32),
            pltpu.VMEM((4, groups * per, block, width + extra), f32),
            pltpu.VMEM((4, groups * per, block, width + extra), f32),
            pltpu.VMEM((nc, width, rows), f32),
            pltpu.VMEM((wide, rows), jnp.bfloat16),
            pltpu.VMEM((wide, rows), jnp.bfloat16),
            pltpu.VMEM((blk, block, width), f32),
            pltpu.VMEM((nc, mc, rows), f32),
            pltpu.VMEM((nc - 1, mc, rows), f32),
            pltpu.VMEM((2, wide, width), f32),
            pltpu.VMEM((2, nw, chunk, width), f32),
            pltpu.VMEM((2, wide, width), f32),
            pltpu.VMEM((mc, 128), f32),
            pltpu.VMEM((nw, mc, 128), f32),
            dma((4,)), dma((4,)), dma,
            dma((4, parts)), dma((4, parts)),
            dma((nc, parts)), dma((nc, parts)),
            dma((nc - 1, parts)), dma((nc - 1, parts)),
            dma((2, nw)), dma((2, nw)),
            dma((nw,)), dma((nw,)),
            dma((nw,)), dma((nw,)),
        ],
        compiler_params=pltpu.CompilerParams(
            collective_id=0, has_side_effects=True, vmem_limit_bytes=56 * 1024 * 1024
        ),
        name="step",
    )(wanted, wanted, search.T, block_values.reshape(blk, block, slots * block), ritz)
    modes_t, resid_t, theta, stiff, mass = pl.pallas_call(
        finish,
        out_shape=tuple(
            jax.ShapeDtypeStruct(shape, f32)
            for shape in ((mc, rows), (mc, rows), (mc,), (width, wide), (width, wide))
        ),
        in_specs=[vmem] * 5,
        out_specs=(vmem,) * 5,
        compiler_params=pltpu.CompilerParams(vmem_limit_bytes=60 * 1024 * 1024),
        name="finish",
    )(*results)
    return modes_t.T, resid_t.T, theta, stiff.T, mass.T


def solution(mesh):
    placed = (P("wire", "col"), P("wire", None), P("wire", None), P())
    return jax.shard_map(
        shards,
        mesh=mesh,
        in_specs=placed,
        out_specs=(P("wire", "col"), P("wire", "col"), P("col"), P(None, "col"), P(None, "col")),
        check_vma=False,
    )
```
